32 devices in a mesh: dp: 4 (over x, core), proto: 8 (over z, y).
Axes of the slice: x: 2, y: 2, z: 4, core: 2. Of those that a mesh axis runs over, the one named last changes fastest.
Arguments:
- student_rows: bfloat16 [5120, 256], P('dp'), may hold values from -0.5 to 0.5
- teacher_rows: bfloat16 [1024, 256], P('dp'), may hold values from -0.5 to 0.5
- prototypes: bfloat16 [256, 4096], P(None, 'proto'), may hold values from -0.375 to 0.375
- crop_image: int32 [5120], P('dp'), may hold values from 0 to 511, as said below
- crop_global: int32 [5120], P('dp'), may hold values from 0 to 2, as said below
Outputs:
- student_grad: float32 [5120, 256], P('dp')
- proto_grad: float32 [256, 4096], P(None, 'proto')
The draws below stay inside these ranges and needn't reach their ends.
Inputs may be any that keep to these rules, and one draw needn't show every extreme that they name: `crop_image`: each image has exactly 10 crops; image i's crops all lie in rows of the aligned block of 1280 rows numbered i // 128, the block of dp that also holds its teacher rows. `crop_global`: for each image exactly one crop has each value 0 to 1 and the others have 2.
All inputs are finite; a program needn't handle non-finite values.
Results may differ from the reference program's by a relative error of at most 0.00065.
The reference program's roundings to bfloat16 on the way count: a program that leaves them out, or rounds other values in their place, can miss the bound.
Values may be sent and summed in bfloat16 or wider, within the bound.
A program may use at most 64 MiB of HBM per device.

```python
import jax
import jax.numpy as jnp
from jax import lax

BOT = 256
IMG_DEV = 128
VIEWS = 10
GLOBALS = 2
ITERS = 3
PROTOS = 4096
IMAGES = 512
CROPS = 5120
TEACH = 1024


def crop_layout(key):
    blocks = IMAGES // IMG_DEV
    block_rows = VIEWS * IMG_DEV
    keys = jax.random.split(key, blocks)
    slots = jax.vmap(lambda k: jax.random.permutation(k, block_rows))(keys)
    offset = (jnp.arange(blocks, dtype=jnp.int32) * IMG_DEV)[:, None]
    image = (offset + slots // VIEWS).reshape(-1).astype(jnp.int32)
    glob = jnp.minimum(slots % VIEWS, GLOBALS).reshape(-1).astype(jnp.int32)
    return (image, glob)


def draw_crop_image(key, part):
    return crop_layout(jax.random.fold_in(key, 7))[0]


def draw_crop_global(key, part):
    return crop_layout(jax.random.fold_in(key, 7))[1]


def level_of(key, shape, cuts, smallest, top_value):
    loudness, own = 1.0, jax.random.fold_in(key, 6)
    for axis_at, blocks in cuts:
        draws = jnp.exp(jax.random.uniform(jax.random.fold_in(own, axis_at), (blocks,), jnp.float32, smallest / len(cuts), top_value / len(cuts)))
        loudness = loudness * jnp.repeat(draws, shape[axis_at] // blocks).reshape([-1 if axis == axis_at else 1 for axis in range(len(shape))])
    return loudness


def bell_draw(rng, extent, width, bound, cuts=(), kind=jnp.bfloat16):
    entries = width * jax.random.normal(rng, extent, jnp.float32)
    if cuts:
        entries = entries * level_of(rng, extent, cuts, -0.22, 0.18)
    return jnp.clip(entries, -bound, bound).astype(kind)


def setup_inputs(seed: int = 0) -> dict:
    seeds = jax.random.split(jax.random.key(seed), 6)
    student_rows = bell_draw(seeds[0], (CROPS, BOT), 0.0625, 0.5, ((0, 4),))
    teacher_rows = bell_draw(seeds[1], (TEACH, BOT), 0.0625, 0.5, ((0, 4),))
    prototypes = bell_draw(seeds[2], (BOT, PROTOS), BOT ** -0.5, 0.375, ((1, 8),))
    crop_image = draw_crop_image(jax.random.fold_in(seeds[5], 71), 0)
    crop_global = draw_crop_global(jax.random.fold_in(seeds[5], 71), 0)
    return {"student_rows": student_rows, "teacher_rows": teacher_rows, "prototypes": prototypes, "crop_image": crop_image, "crop_global": crop_global}


def unit_rows(rows):
    scale = lax.rsqrt(lax.optimization_barrier(jnp.sum(rows * rows, axis=1, keepdims=True)) + 1e-06)
    return (rows * scale, scale)

def reference(student_rows, teacher_rows, prototypes, crop_image, crop_global):
    weights = prototypes.astype(jnp.float32)
    col_scale = lax.rsqrt(lax.optimization_barrier(jnp.sum(weights * weights, axis=0, keepdims=True)) + 1e-06)
    w_norm = weights * col_scale
    w_bf = w_norm.astype(jnp.bfloat16)
    t_norm, t_scale = unit_rows(teacher_rows.astype(jnp.float32))
    t_bf = t_norm.astype(jnp.bfloat16)
    q_mat = jnp.exp(jnp.dot(t_bf, w_bf, preferred_element_type=jnp.float32) / 0.07)
    for step in range(ITERS):
        q_mat = q_mat / lax.optimization_barrier(jnp.sum(q_mat, axis=0, keepdims=True)) / PROTOS
        q_mat = q_mat / lax.optimization_barrier(jnp.sum(q_mat, axis=1, keepdims=True)) / TEACH
    targets = q_mat * TEACH
    x_norm, x_scale = unit_rows(student_rows.astype(jnp.float32))
    x_bf = x_norm.astype(jnp.bfloat16)
    block_rows = VIEWS * IMG_DEV
    blocks = CROPS // block_rows
    scale_out = PROTOS / 64.0

    def one_block(carry, index):
        start = (index * block_rows).astype(jnp.int32)
        xb_blk = lax.dynamic_slice_in_dim(x_bf, start, block_rows, 0)
        xn_blk = lax.dynamic_slice_in_dim(x_norm, start, block_rows, 0)
        xr_blk = lax.dynamic_slice_in_dim(x_scale, start, block_rows, 0)
        image_blk = lax.dynamic_slice_in_dim(crop_image, start, block_rows, 0)
        glob_blk = lax.dynamic_slice_in_dim(crop_global, start, block_rows, 0)
        logits = jnp.dot(xb_blk, w_bf, preferred_element_type=jnp.float32) / 0.1
        expo = jnp.exp(logits)
        total = lax.optimization_barrier(jnp.sum(expo, axis=1, keepdims=True))
        probs = expo / total
        first = jnp.take(targets, GLOBALS * image_blk, axis=0)
        second = jnp.take(targets, GLOBALS * image_blk + 1, axis=0)
        keep_first = (glob_blk != 0).astype(jnp.float32)[:, None]
        keep_second = (glob_blk != 1).astype(jnp.float32)[:, None]
        target_blk = first * keep_first + second * keep_second
        count = keep_first + keep_second
        grad_bf = (scale_out * (count * probs - target_blk) / 0.1).astype(jnp.bfloat16)
        dxn = lax.dot_general(grad_bf, w_bf, (((1,), (1,)), ((), ())), preferred_element_type=jnp.float32)
        dx_blk = xr_blk * (dxn - xn_blk * lax.optimization_barrier(jnp.sum(xn_blk * dxn, axis=1, keepdims=True)))
        dwn = lax.dot_general(xb_blk, grad_bf, (((0,), (0,)), ((), ())), preferred_element_type=jnp.float32)
        return (carry + dwn, dx_blk)
    dwn_total, dx_all = lax.scan(one_block, jnp.zeros((BOT, PROTOS), jnp.float32), jnp.arange(blocks, dtype=jnp.int32))
    student_grad = dx_all.reshape(CROPS, BOT)
    proto_grad = col_scale * (dwn_total - w_norm * lax.optimization_barrier(jnp.sum(w_norm * dwn_total, axis=0, keepdims=True)))
    return (student_grad, proto_grad)
```

```python
import functools

import jax
import jax.numpy as jnp
from jax import lax
from jax.experimental import pallas as pl
from jax.experimental.pallas import tpu as pltpu
from jax.sharding import PartitionSpec as P

GLOBALS = 2
ITERS = 3
MESH = pl.DeviceIdType.MESH
F32 = jnp.float32
BF16 = jnp.bfloat16
VMEM_BUDGET = 52 * 2**20
VMEM_LIMIT = 60 * 2**20


def unit_rows(rows):
    scale = lax.rsqrt(jnp.sum(rows * rows, axis=1, keepdims=True) + 1e-06)
    return (rows * scale, scale)


def fold_lanes(block):
    total = block[:, :128]
    for at in range(128, block.shape[1], 128):
        total = total + block[:, at : at + 128]
    return total


def head_kernel(
    nd, npr, tile,
    x_ref, t_ref, w_ref, img_ref, glob_ref, dx_ref, dw_ref,
    wraw, wn, q, e, tt, s2, xb, zacc, a_ref, cs, cvec, dwp, dwa, dwb, dwc, dwf,
    wsend, wrecv, csend, crecv, dsend, drecv,
):
    me_d, me_p = lax.axis_index("dp"), lax.axis_index("proto")
    crops, bot = x_ref.shape
    teach = t_ref.shape[0]
    protos = w_ref.shape[1]
    tiles = crops // tile
    gain = (npr * protos / 64.0) / 0.1
    quarter = bot // nd
    half = bot // 2
    core_d = me_d + 1 - 2 * (me_d % 2)
    far_d = (me_d + nd // 2) % nd
    diag_d = (core_d + nd // 2) % nd
    flip = lambda b: b + 1 - 2 * (b % 2)
    y_p = flip(me_p)
    z_ps = [(me_p + 2 * k) % npr for k in range(1, npr // 2)]

    barrier = pltpu.get_barrier_semaphore()
    peers = [(me_d, p) for p in z_ps + [y_p]] + [(d, me_p) for d in (core_d, far_d, diag_d)]
    for peer in peers:
        pl.semaphore_signal(barrier, inc=1, device_id=peer, device_id_type=MESH)
    pl.semaphore_wait(barrier, len(peers))

    started = []

    def rows_of(which):
        return pl.ds(pl.multiple_of(which * quarter, quarter), quarter)

    def send_w(src, block, which, target):
        copy = pltpu.make_async_remote_copy(
            src_ref=src,
            dst_ref=wraw.at[block, rows_of(which)],
            send_sem=wsend.at[len(started)],
            recv_sem=wrecv.at[block, which],
            device_id=target,
            device_id_type=MESH,
        )
        copy.start()
        started.append(copy)

    def arrived(block, which):
        here = wraw.at[block, rows_of(which)]
        pltpu.make_async_remote_copy(
            src_ref=here, dst_ref=here, send_sem=wsend.at[0], recv_sem=wrecv.at[block, which],
            device_id=(core_d, me_p), device_id_type=MESH,
        ).wait_recv()

    def pass_w(block, which, target):
        send_w(wraw.at[block, rows_of(which)], block, which, target)

    own_part = w_ref.at[rows_of(me_d)]
    for p in z_ps + [y_p]:
        send_w(own_part, me_p, me_d, (me_d, p))

    t_b = unit_rows(t_ref[...].astype(F32))[0].astype(BF16)

    def ready(block, raw):
        w = raw.astype(F32)
        w_b = (w * lax.rsqrt(jnp.sum(w * w, axis=0, keepdims=True) + 1e-06)).astype(BF16)
        wn[block] = w_b
        q_b = jnp.exp(jnp.dot(t_b, w_b, preferred_element_type=F32) / 0.07)
        q[block] = q_b
        cs[0, me_d, pl.ds(block, 1), :] = jnp.sum(q_b, axis=0, keepdims=True)

    ready(me_p, w_ref[...])

    order = [y_p] + z_ps + [flip(p) for p in z_ps]
    for at, block in enumerate(order):
        arrived(block, me_d)
        if 1 <= at <= len(z_ps):
            pass_w(block, me_d, (me_d, y_p))
        pass_w(block, me_d, (far_d, me_p))
        pass_w(block, me_d, (core_d, me_p))

    offset = me_d * (teach // GLOBALS)

    @pl.loop(0, tiles)
    def _(i):
        at = pl.multiple_of(i * tile, tile)
        rows = pl.ds(at, tile)
        xb[rows, :] = unit_rows(x_ref[rows, :].astype(F32))[0].astype(BF16)
        image = (img_ref[:, rows] - offset) * GLOBALS
        glob = glob_ref[:, rows]
        slot = lax.broadcasted_iota(jnp.int32, (teach, tile), 0)
        pick = jnp.zeros((teach, tile), F32)
        for v in range(GLOBALS):
            pick = pick + jnp.where((slot == image + v) & (glob != v), 1.0, 0.0)
        pick = jnp.transpose(pick)
        s2[rows, :teach] = pick.astype(BF16)
        s2[rows, teach:] = pick.astype(BF16)
        a_ref[rows, :] = jnp.broadcast_to(jnp.sum(pick, axis=1, keepdims=True), (tile, 128))
        zacc[rows, :] = jnp.zeros((tile, 128), F32)

    for block in order:
        arrived(block, far_d)
        pass_w(block, far_d, (core_d, me_p))
    for block in order:
        arrived(block, core_d)
        arrived(block, diag_d)
        ready(block, wraw[block])

    def student_block(b):
        @pl.loop(0, tiles)
        def _(i):
            rows = pl.ds(pl.multiple_of(i * tile, tile), tile)
            expo = jnp.exp(jnp.dot(xb[rows, :], wn[b], preferred_element_type=F32) / 0.1)
            e[b, rows, :] = expo
            zacc[rows, :] += fold_lanes(expo)

    def row_scale():
        def body(b, acc):
            return acc + fold_lanes(q[b] * cvec[pl.ds(b, 1), :])
        acc = lax.fori_loop(0, npr, body, jnp.zeros((teach, 128), F32))
        return 1.0 / jnp.sum(acc, axis=1, keepdims=True)

    cuts = [npr * k // ITERS for k in range(ITERS + 1)]
    for step in range(ITERS):
        if step:
            r = row_scale()

            @pl.loop(0, npr)
            def _(b):
                cs[step, me_d, pl.ds(b, 1), :] = jnp.sum(q[b] * r, axis=0, keepdims=True)

        copies = []
        for k, d in enumerate((core_d, far_d, diag_d)):
            copy = pltpu.make_async_remote_copy(
                src_ref=cs.at[step, me_d],
                dst_ref=cs.at[step, me_d],
                send_sem=csend.at[step, k],
                recv_sem=crecv.at[step, k],
                device_id=(d, me_p),
                device_id_type=MESH,
            )
            copy.start()
            copies.append(copy)
        pl.loop(cuts[step], cuts[step + 1])(student_block)
        for copy in copies:
            copy.wait()
        total = cs[step, 0]
        for d in range(1, nd):
            total = total + cs[step, d]
        cvec[...] = 1.0 / total
    r = row_scale() * gain

    @pl.loop(0, npr)
    def _(b):
        target = q[b] * r * cvec[pl.ds(b, 1), :]
        high = target.astype(BF16)
        tt[b, :teach, :] = high
        tt[b, teach:, :] = (target - high.astype(F32)).astype(BF16)

    def grad(b, rows):
        target = jnp.dot(s2[rows, :], tt[b], preferred_element_type=F32)
        return (e[b, rows, :] * a_ref[rows, 0:1] - target).astype(BF16)

    dwp[...] = jnp.zeros_like(dwp)

    @pl.loop(0, tiles)
    def _(i):
        rows = pl.ds(pl.multiple_of(i * tile, tile), tile)
        a_ref[rows, :] = jnp.broadcast_to(
            a_ref[rows, 0:1] * gain / jnp.sum(zacc[rows, :], axis=1, keepdims=True), (tile, 128)
        )
        dwp[...] += lax.dot_general(
            xb[rows, :], grad(me_p, rows), (((0,), (0,)), ((), ())), preferred_element_type=F32
        )

    def part(which):
        return pl.ds(pl.multiple_of(which * half, half), half)

    mine, other = me_d % 2, 1 - me_d % 2

    def send_d(k, src, dst, d):
        copy = pltpu.make_async_remote_copy(
            src_ref=src, dst_ref=dst, send_sem=dsend.at[k], recv_sem=drecv.at[k],
            device_id=(d, me_p), device_id_type=MESH,
        )
        copy.start()
        return copy

    def student_rows(first, last):
        @pl.loop(first, last)
        def _(i):
            rows = pl.ds(pl.multiple_of(i * tile, tile), tile)
            dx_ref[rows, :] = jnp.zeros((tile, bot), F32)

            @pl.loop(0, npr)
            def _(b):
                dx_ref[rows, :] += lax.dot_general(
                    grad(b, rows), wn[b], (((1,), (1,)), ((), ())), preferred_element_type=F32
                )

            x_n, x_r = unit_rows(x_ref[rows, :].astype(F32))
            dxn = dx_ref[rows, :]
            dx_ref[rows, :] = x_r * (dxn - x_n * jnp.sum(x_n * dxn, axis=1, keepdims=True))

    first = send_d(0, dwp.at[part(other)], dwa, core_d)
    student_rows(0, tiles // 4)
    first.wait()
    dwb[...] = dwp[part(mine), :] + dwa[...]
    second = send_d(1, dwb, dwc, far_d)
    student_rows(tiles // 4, tiles - 1)
    second.wait()
    dwf[part(mine), :] = dwb[...] + dwc[...]
    third = send_d(2, dwf.at[part(mine)], dwf.at[part(mine)], core_d)
    student_rows(tiles - 1, tiles)
    third.wait()
    w = w_ref[...].astype(F32)
    v_r = lax.rsqrt(jnp.sum(w * w, axis=0, keepdims=True) + 1e-06)
    w_n = w * v_r
    dwn = dwf[...]
    dw_ref[...] = v_r * (dwn - w_n * jnp.sum(w_n * dwn, axis=0, keepdims=True))
    for copy in started:
        copy.wait_send()


def row_tile(crops):
    return next((t for t in (256, 128) if crops % t == 0), 0)


def scratch_of(nd, npr, crops, bot, teach, protos):
    links = nd * (npr - 1)
    return [
        ((npr, bot, protos), BF16),
        ((npr, bot, protos), BF16),
        ((npr, teach, protos), F32),
        ((npr, crops, protos), F32),
        ((npr, 2 * teach, protos), BF16),
        ((crops, 2 * teach), BF16),
        ((crops, bot), BF16),
        ((crops, 128), F32),
        ((crops, 128), F32),
        ((ITERS, nd, npr, protos), F32),
        ((npr, protos), F32),
        ((bot, protos), F32),
        ((bot // 2, protos), F32),
        ((bot // 2, protos), F32),
        ((bot // 2, protos), F32),
        ((bot, protos), F32),
    ], links


def fused(student_rows, teacher_rows, prototypes, crop_image, crop_global):
    nd, npr = lax.axis_size("dp"), lax.axis_size("proto")
    crops, bot = student_rows.shape
    teach, protos = teacher_rows.shape[0], prototypes.shape[1]
    shapes, links = scratch_of(nd, npr, crops, bot, teach, protos)
    whole = pl.BlockSpec(memory_space=pltpu.VMEM)
    return pl.pallas_call(
        functools.partial(head_kernel, nd, npr, row_tile(crops)),
        out_shape=(
            jax.ShapeDtypeStruct((crops, bot), F32),
            jax.ShapeDtypeStruct((bot, protos), F32),
        ),
        in_specs=[whole] * 5,
        out_specs=(whole, whole),
        scratch_shapes=[pltpu.VMEM(shape, kind) for shape, kind in shapes]
        + [
            pltpu.SemaphoreType.DMA((links,)),
            pltpu.SemaphoreType.DMA((npr, nd)),
            pltpu.SemaphoreType.DMA((ITERS, nd - 1)),
            pltpu.SemaphoreType.DMA((ITERS, nd - 1)),
            pltpu.SemaphoreType.DMA((3,)),
            pltpu.SemaphoreType.DMA((3,)),
        ],
        compiler_params=pltpu.CompilerParams(
            collective_id=0, has_side_effects=True, vmem_limit_bytes=VMEM_LIMIT
        ),
        cost_estimate=pl.CostEstimate(
            flops=10 * crops * npr * protos * bot,
            bytes_accessed=4 * (crops * bot + bot * protos),
            transcendentals=npr * protos * (crops + teach),
        ),
    )(student_rows, teacher_rows, prototypes, crop_image.reshape(1, -1), crop_global.reshape(1, -1))


def fits(nd, npr, crops, bot, teach, protos):
    shapes, _ = scratch_of(nd, npr, crops, bot, teach, protos)
    size = 0
    for shape, kind in shapes:
        count = 1
        for extent in shape:
            count *= extent
        size += count * jnp.dtype(kind).itemsize
    tiled = row_tile(crops) and protos % 128 == 0 and bot % (nd * 16) == 0 and teach % 128 == 0
    return nd == 4 and npr % 2 == 0 and bool(tiled) and size <= VMEM_BUDGET


def on_device(student_rows, teacher_rows, prototypes, crop_image, crop_global):
    sizes = (*student_rows.shape, teacher_rows.shape[0], prototypes.shape[1])
    if fits(lax.axis_size("dp"), lax.axis_size("proto"), *sizes):
        return fused(student_rows, teacher_rows, prototypes, crop_image, crop_global)
    total_protos = lax.axis_size("proto") * prototypes.shape[1]
    img_local = teacher_rows.shape[0] // GLOBALS
    teach_total = lax.axis_size("dp") * teacher_rows.shape[0]
    weights = prototypes.astype(jnp.float32)
    col_scale = lax.rsqrt(jnp.sum(weights * weights, axis=0, keepdims=True) + 1e-06)
    w_norm = weights * col_scale
    w_bf = w_norm.astype(jnp.bfloat16)
    t_norm, t_scale = unit_rows(teacher_rows.astype(jnp.float32))
    t_bf = t_norm.astype(jnp.bfloat16)
    q_mat = jnp.exp(jnp.dot(t_bf, w_bf, preferred_element_type=jnp.float32) / 0.07)
    for step in range(ITERS):
        q_mat = q_mat / lax.psum(jnp.sum(q_mat, axis=0), "dp")[None, :] / total_protos
        row_tot = lax.psum(jnp.sum(q_mat, axis=1), "proto")
        q_mat = q_mat / row_tot[:, None] / teach_total
    targets = q_mat * teach_total
    x_norm, x_scale = unit_rows(student_rows.astype(jnp.float32))
    x_bf = x_norm.astype(jnp.bfloat16)
    logits = jnp.dot(x_bf, w_bf, preferred_element_type=jnp.float32) / 0.1
    expo = jnp.exp(logits)
    total = lax.psum(jnp.sum(expo, axis=1), "proto")
    probs = expo / total[:, None]
    image_here = crop_image - lax.axis_index("dp") * img_local
    first = jnp.take(targets, GLOBALS * image_here, axis=0)
    second = jnp.take(targets, GLOBALS * image_here + 1, axis=0)
    keep_first = (crop_global != 0).astype(jnp.float32)[:, None]
    keep_second = (crop_global != 1).astype(jnp.float32)[:, None]
    target_rows = first * keep_first + second * keep_second
    count = keep_first + keep_second
    scale_out = total_protos / 64.0
    grad_bf = (scale_out * (count * probs - target_rows) / 0.1).astype(jnp.bfloat16)
    crops_here = grad_bf.shape[0]
    groups = lax.axis_size("proto")
    share = -(-crops_here // groups)
    dxn_share = lax.psum_scatter(
        lax.dot_general(
            grad_bf, w_bf, (((1,), (1,)), ((), ())), preferred_element_type=jnp.float32
        ),
        "proto",
        scatter_dimension=0,
        tiled=True,
    )
    begin = lax.axis_index("proto") * share
    xn_share = lax.dynamic_slice_in_dim(x_norm, begin, share, 0)
    xr_share = lax.dynamic_slice_in_dim(x_scale, begin, share, 0)
    dx_share = xr_share * (
        dxn_share - xn_share * jnp.sum(xn_share * dxn_share, axis=1, keepdims=True)
    )
    student_grad = lax.all_gather(dx_share, "proto", axis=0, tiled=True)
    dwn_local = lax.dot_general(
        x_bf, grad_bf, (((0,), (0,)), ((), ())), preferred_element_type=jnp.float32
    )
    dwn_total = lax.psum(dwn_local, "dp")
    proto_grad = col_scale * (
        dwn_total - w_norm * jnp.sum(w_norm * dwn_total, axis=0, keepdims=True)
    )
    return (student_grad, proto_grad)


def solution(mesh):
    placed = (P("dp", None), P("dp", None), P(None, "proto"), P("dp"), P("dp"))
    return jax.shard_map(
        on_device,
        mesh=mesh,
        in_specs=placed,
        out_specs=(P("dp", None), P(None, "proto")),
        check_vma=False,
    )
```

```python
import functools
import math

import jax
import jax.numpy as jnp
from jax import lax
from jax.experimental import pallas as pl
from jax.experimental.pallas import tpu as pltpu
from jax.sharding import PartitionSpec as P

GLOBALS = 2
ITERS = 3
LOG2E = math.log2(math.e)
MESH = pl.DeviceIdType.MESH
F32 = jnp.float32
BF16 = jnp.bfloat16
VMEM_BUDGET = 52 * 2**20
VMEM_LIMIT = 60 * 2**20


def unit_rows(rows):
    scale = lax.rsqrt(jnp.sum(rows * rows, axis=1, keepdims=True) + 1e-06)
    return (rows * scale, scale)


def fold_lanes(block):
    total = block[:, :128]
    for at in range(128, block.shape[1], 128):
        total = total + block[:, at : at + 128]
    return total


def head_kernel(
    nd, npr, tile,
    x_ref, t_ref, w_ref, img_ref, glob_ref, dx_ref, dw_ref,
    wraw, wn, q, e, tt, s2, xb, zacc, a_ref, cs, cvec, dwp, dwa, dwb, dwc, dwf,
    wsend, wrecv, csend, crecv, dsend, drecv,
):
    me_d, me_p = lax.axis_index("dp"), lax.axis_index("proto")
    crops, bot = x_ref.shape
    teach = t_ref.shape[0]
    protos = w_ref.shape[1]
    tiles = crops // tile
    gain = (npr * protos / 64.0) / 0.1
    quarter = bot // nd
    half = bot // 2
    core_d = me_d + 1 - 2 * (me_d % 2)
    far_d = (me_d + nd // 2) % nd
    diag_d = (core_d + nd // 2) % nd
    flip = lambda b: b + 1 - 2 * (b % 2)
    y_p = flip(me_p)
    z_ps = [(me_p + 2 * k) % npr for k in range(1, npr // 2)]

    barrier = pltpu.get_barrier_semaphore()
    peers = [(me_d, p) for p in z_ps + [y_p]] + [(d, me_p) for d in (core_d, far_d, diag_d)]
    for peer in peers:
        pl.semaphore_signal(barrier, inc=1, device_id=peer, device_id_type=MESH)
    pl.semaphore_wait(barrier, len(peers))

    started = []

    def rows_of(which):
        return pl.ds(pl.multiple_of(which * quarter, quarter), quarter)

    def send_w(src, block, which, target):
        copy = pltpu.make_async_remote_copy(
            src_ref=src,
            dst_ref=wraw.at[block, rows_of(which)],
            send_sem=wsend.at[len(started)],
            recv_sem=wrecv.at[block, which],
            device_id=target,
            device_id_type=MESH,
        )
        copy.start()
        started.append(copy)

    def arrived(block, which):
        here = wraw.at[block, rows_of(which)]
        pltpu.make_async_remote_copy(
            src_ref=here, dst_ref=here, send_sem=wsend.at[0], recv_sem=wrecv.at[block, which],
            device_id=(core_d, me_p), device_id_type=MESH,
        ).wait_recv()

    def pass_w(block, which, target):
        send_w(wraw.at[block, rows_of(which)], block, which, target)

    own_part = w_ref.at[rows_of(me_d)]
    for p in z_ps + [y_p]:
        send_w(own_part, me_p, me_d, (me_d, p))

    t_b = unit_rows(t_ref[...].astype(F32))[0].astype(BF16)

    def ready(block, raw):
        w = raw.astype(F32)
        w_b = (w * lax.rsqrt(jnp.sum(w * w, axis=0, keepdims=True) + 1e-06)).astype(BF16)
        wn[block] = w_b
        q_b = jnp.exp2(jnp.dot(t_b, w_b, preferred_element_type=F32) * (LOG2E / 0.07))
        q[block] = q_b
        cs[0, me_d, pl.ds(block, 1), :] = jnp.sum(q_b, axis=0, keepdims=True)

    def student_block(b):
        @pl.loop(0, tiles)
        def _(i):
            rows = pl.ds(pl.multiple_of(i * tile, tile), tile)
            logits = jnp.dot(xb[rows, :], wn[b], preferred_element_type=F32)
            expo = jnp.exp2(logits * (LOG2E / 0.1))
            e[b, rows, :] = expo
            zacc[b, rows, :] = fold_lanes(expo)

    def normalize_students():
        @pl.loop(0, tiles)
        def _(i):
            rows = pl.ds(pl.multiple_of(i * tile, tile), tile)
            xb[rows, :] = unit_rows(x_ref[rows, :].astype(F32))[0].astype(BF16)

    def pick_targets():
        offset = me_d * (teach // GLOBALS)
        image = (img_ref[...].reshape(1, crops) - offset) * GLOBALS
        glob = glob_ref[...].reshape(1, crops)
        width = 256 if crops % 256 == 0 else 128
        for at in range(0, crops, width):
            rows = slice(at, at + width)
            slot = lax.broadcasted_iota(jnp.int32, (teach, width), 0)
            pick = jnp.zeros((teach, width), F32)
            for v in range(GLOBALS):
                here = (slot == image[:, rows] + v) & (glob[:, rows] != v)
                pick = pick + jnp.where(here, 1.0, 0.0)
            pick = jnp.transpose(pick)
            s2[rows, :teach] = pick.astype(BF16)
            s2[rows, teach:] = pick.astype(BF16)
            count = jnp.sum(pick, axis=1, keepdims=True)
            a_ref[rows, :] = jnp.broadcast_to(count, (width, 128))

    order = [y_p] + z_ps + [flip(p) for p in z_ps]

    def relay(at):
        block = order[at]
        arrived(block, me_d)
        if 1 <= at <= len(z_ps):
            pass_w(block, me_d, (me_d, y_p))
        pass_w(block, me_d, (far_d, me_p))
        pass_w(block, me_d, (core_d, me_p))

    def share(at):
        arrived(order[at], far_d)
        pass_w(order[at], far_d, (core_d, me_p))

    def take(at):
        block = order[at]
        arrived(block, core_d)
        arrived(block, diag_d)
        ready(block, wraw[block])

    ready(me_p, w_ref[...])
    count = len(order)
    relay(0)
    normalize_students()
    for at in range(1, len(z_ps) + 1):
        relay(at)
    student_block(me_p)
    share(0)
    later = count - ITERS
    for at in range(count):
        if at + len(z_ps) + 1 < count:
            relay(at + len(z_ps) + 1)
        if at + 1 < count:
            share(at + 1)
        take(at)
        if at < later:
            student_block(order[at])

    def row_scale():
        def body(b, acc):
            return acc + fold_lanes(q[b] * cvec[pl.ds(b, 1), :])
        acc = lax.fori_loop(0, npr, body, jnp.zeros((teach, 128), F32))
        return 1.0 / jnp.sum(acc, axis=1, keepdims=True)

    for step in range(ITERS):
        if step:
            r = row_scale()

            @pl.loop(0, npr)
            def _(b):
                cs[step, me_d, pl.ds(b, 1), :] = jnp.sum(q[b] * r, axis=0, keepdims=True)

        copies = []
        for k, d in enumerate((core_d, far_d, diag_d)):
            copy = pltpu.make_async_remote_copy(
                src_ref=cs.at[step, me_d],
                dst_ref=cs.at[step, me_d],
                send_sem=csend.at[step, k],
                recv_sem=crecv.at[step, k],
                device_id=(d, me_p),
                device_id_type=MESH,
            )
            copy.start()
            copies.append(copy)
        student_block(order[later + step])
        if step == 0:
            pick_targets()
        for copy in copies:
            copy.wait()
        total = cs[step, 0]
        for d in range(1, nd):
            total = total + cs[step, d]
        cvec[...] = 1.0 / total
    r = row_scale() * gain

    @pl.loop(0, npr)
    def _(b):
        target = q[b] * r * cvec[pl.ds(b, 1), :]
        high = target.astype(BF16)
        tt[b, :teach, :] = high
        tt[b, teach:, :] = (target - high.astype(F32)).astype(BF16)

    def grad(b, rows):
        target = jnp.dot(s2[rows, :], tt[b], preferred_element_type=F32)
        scale = jnp.concatenate([a_ref[rows, :]] * (protos // 128), axis=1)
        return (e[b, rows, :] * scale - target).astype(BF16)

    dwp[...] = jnp.zeros_like(dwp)

    @pl.loop(0, tiles)
    def _(i):
        rows = pl.ds(pl.multiple_of(i * tile, tile), tile)
        z = zacc[0, rows, :]
        for b in range(1, npr):
            z = z + zacc[b, rows, :]
        a_ref[rows, :] = a_ref[rows, :] * (gain / jnp.sum(z, axis=1, keepdims=True))
        dwp[...] += lax.dot_general(
            xb[rows, :], grad(me_p, rows), (((0,), (0,)), ((), ())), preferred_element_type=F32
        )

    def part(which):
        return pl.ds(pl.multiple_of(which * half, half), half)

    mine, other = me_d % 2, 1 - me_d % 2

    def send_d(k, src, dst, d):
        copy = pltpu.make_async_remote_copy(
            src_ref=src, dst_ref=dst, send_sem=dsend.at[k], recv_sem=drecv.at[k],
            device_id=(d, me_p), device_id_type=MESH,
        )
        copy.start()
        return copy

    def student_sums(first, last):
        @pl.loop(first, last)
        def _(b):
            @pl.loop(0, tiles)
            def _(i):
                rows = pl.ds(pl.multiple_of(i * tile, tile), tile)
                dx_ref[rows, :] += lax.dot_general(
                    grad(b, rows), wn[b], (((1,), (1,)), ((), ())), preferred_element_type=F32
                )

    first = send_d(0, dwp.at[part(other)], dwa, core_d)
    dx_ref[...] = jnp.zeros_like(dx_ref)
    student_sums(0, npr // 4)
    first.wait()
    dwb[...] = dwp[part(mine), :] + dwa[...]
    second = send_d(1, dwb, dwc, far_d)
    student_sums(npr // 4, npr)
    second.wait()
    dwf[part(mine), :] = dwb[...] + dwc[...]
    third = send_d(2, dwf.at[part(mine)], dwf.at[part(mine)], core_d)

    @pl.loop(0, tiles)
    def _(i):
        rows = pl.ds(pl.multiple_of(i * tile, tile), tile)
        x_n, x_r = unit_rows(x_ref[rows, :].astype(F32))
        dxn = dx_ref[rows, :]
        dx_ref[rows, :] = x_r * (dxn - x_n * jnp.sum(x_n * dxn, axis=1, keepdims=True))

    third.wait()
    w = w_ref[...].astype(F32)
    v_r = lax.rsqrt(jnp.sum(w * w, axis=0, keepdims=True) + 1e-06)
    w_n = w * v_r
    dwn = dwf[...]
    dw_ref[...] = v_r * (dwn - w_n * jnp.sum(w_n * dwn, axis=0, keepdims=True))
    for copy in started:
        copy.wait_send()


def row_tile(crops):
    return next((t for t in (640, 512, 256, 128) if crops % t == 0), 0)


def scratch_of(nd, npr, crops, bot, teach, protos):
    links = nd * (npr - 1)
    return [
        ((npr, bot, protos), BF16),
        ((npr, bot, protos), BF16),
        ((npr, teach, protos), F32),
        ((npr, crops, protos), F32),
        ((npr, 2 * teach, protos), BF16),
        ((crops, 2 * teach), BF16),
        ((crops, bot), BF16),
        ((npr, crops, 128), F32),
        ((crops, 128), F32),
        ((ITERS, nd, npr, protos), F32),
        ((npr, protos), F32),
        ((bot, protos), F32),
        ((bot // 2, protos), F32),
        ((bot // 2, protos), F32),
        ((bot // 2, protos), F32),
        ((bot, protos), F32),
    ], links


def fused(student_rows, teacher_rows, prototypes, crop_image, crop_global):
    nd, npr = lax.axis_size("dp"), lax.axis_size("proto")
    crops, bot = student_rows.shape
    teach, protos = teacher_rows.shape[0], prototypes.shape[1]
    shapes, links = scratch_of(nd, npr, crops, bot, teach, protos)
    whole = pl.BlockSpec(memory_space=pltpu.VMEM)
    return pl.pallas_call(
        functools.partial(head_kernel, nd, npr, row_tile(crops)),
        out_shape=(
            jax.ShapeDtypeStruct((crops, bot), F32),
            jax.ShapeDtypeStruct((bot, protos), F32),
        ),
        in_specs=[whole] * 5,
        out_specs=(whole, whole),
        scratch_shapes=[pltpu.VMEM(shape, kind) for shape, kind in shapes]
        + [
            pltpu.SemaphoreType.DMA((links,)),
            pltpu.SemaphoreType.DMA((npr, nd)),
            pltpu.SemaphoreType.DMA((ITERS, nd - 1)),
            pltpu.SemaphoreType.DMA((ITERS, nd - 1)),
            pltpu.SemaphoreType.DMA((3,)),
            pltpu.SemaphoreType.DMA((3,)),
        ],
        compiler_params=pltpu.CompilerParams(
            collective_id=0, has_side_effects=True, vmem_limit_bytes=VMEM_LIMIT
        ),
        cost_estimate=pl.CostEstimate(
            flops=10 * crops * npr * protos * bot,
            bytes_accessed=4 * (crops * bot + bot * protos),
            transcendentals=npr * protos * (crops + teach),
        ),
    )(student_rows, teacher_rows, prototypes, crop_image, crop_global)


def fits(nd, npr, crops, bot, teach, protos):
    shapes, _ = scratch_of(nd, npr, crops, bot, teach, protos)
    size = 0
    for shape, kind in shapes:
        count = 1
        for extent in shape:
            count *= extent
        size += count * jnp.dtype(kind).itemsize
    tiled = row_tile(crops) and protos % 128 == 0 and bot % (nd * 16) == 0 and teach % 128 == 0
    return nd == 4 and npr % 2 == 0 and npr > ITERS and bool(tiled) and size <= VMEM_BUDGET


def on_device(student_rows, teacher_rows, prototypes, crop_image, crop_global):
    sizes = (*student_rows.shape, teacher_rows.shape[0], prototypes.shape[1])
    if fits(lax.axis_size("dp"), lax.axis_size("proto"), *sizes):
        return fused(student_rows, teacher_rows, prototypes, crop_image, crop_global)
    total_protos = lax.axis_size("proto") * prototypes.shape[1]
    img_local = teacher_rows.shape[0] // GLOBALS
    teach_total = lax.axis_size("dp") * teacher_rows.shape[0]
    weights = prototypes.astype(jnp.float32)
    col_scale = lax.rsqrt(jnp.sum(weights * weights, axis=0, keepdims=True) + 1e-06)
    w_norm = weights * col_scale
    w_bf = w_norm.astype(jnp.bfloat16)
    t_norm, t_scale = unit_rows(teacher_rows.astype(jnp.float32))
    t_bf = t_norm.astype(jnp.bfloat16)
    q_mat = jnp.exp(jnp.dot(t_bf, w_bf, preferred_element_type=jnp.float32) / 0.07)
    for step in range(ITERS):
        q_mat = q_mat / lax.psum(jnp.sum(q_mat, axis=0), "dp")[None, :] / total_protos
        row_tot = lax.psum(jnp.sum(q_mat, axis=1), "proto")
        q_mat = q_mat / row_tot[:, None] / teach_total
    targets = q_mat * teach_total
    x_norm, x_scale = unit_rows(student_rows.astype(jnp.float32))
    x_bf = x_norm.astype(jnp.bfloat16)
    logits = jnp.dot(x_bf, w_bf, preferred_element_type=jnp.float32) / 0.1
    expo = jnp.exp(logits)
    total = lax.psum(jnp.sum(expo, axis=1), "proto")
    probs = expo / total[:, None]
    image_here = crop_image - lax.axis_index("dp") * img_local
    first = jnp.take(targets, GLOBALS * image_here, axis=0)
    second = jnp.take(targets, GLOBALS * image_here + 1, axis=0)
    keep_first = (crop_global != 0).astype(jnp.float32)[:, None]
    keep_second = (crop_global != 1).astype(jnp.float32)[:, None]
    target_rows = first * keep_first + second * keep_second
    count = keep_first + keep_second
    scale_out = total_protos / 64.0
    grad_bf = (scale_out * (count * probs - target_rows) / 0.1).astype(jnp.bfloat16)
    crops_here = grad_bf.shape[0]
    groups = lax.axis_size("proto")
    share = -(-crops_here // groups)
    dxn_share = lax.psum_scatter(
        lax.dot_general(
            grad_bf, w_bf, (((1,), (1,)), ((), ())), preferred_element_type=jnp.float32
        ),
        "proto",
        scatter_dimension=0,
        tiled=True,
    )
    begin = lax.axis_index("proto") * share
    xn_share = lax.dynamic_slice_in_dim(x_norm, begin, share, 0)
    xr_share = lax.dynamic_slice_in_dim(x_scale, begin, share, 0)
    dx_share = xr_share * (
        dxn_share - xn_share * jnp.sum(xn_share * dxn_share, axis=1, keepdims=True)
    )
    student_grad = lax.all_gather(dx_share, "proto", axis=0, tiled=True)
    dwn_local = lax.dot_general(
        x_bf, grad_bf, (((0,), (0,)), ((), ())), preferred_element_type=jnp.float32
    )
    dwn_total = lax.psum(dwn_local, "dp")
    proto_grad = col_scale * (
        dwn_total - w_norm * jnp.sum(w_norm * dwn_total, axis=0, keepdims=True)
    )
    return (student_grad, proto_grad)


def solution(mesh):
    placed = (P("dp", None), P("dp", None), P(None, "proto"), P("dp"), P("dp"))
    return jax.shard_map(
        on_device,
        mesh=mesh,
        in_specs=placed,
        out_specs=(P("dp", None), P(None, "proto")),
        check_vma=False,
    )
```

```python
import functools
import math

import jax
import jax.numpy as jnp
from jax import lax
from jax.experimental import pallas as pl
from jax.experimental.pallas import tpu as pltpu
from jax.sharding import PartitionSpec as P

GLOBALS = 2
ITERS = 3
LOG2E = math.log2(math.e)
MESH = pl.DeviceIdType.MESH
F32 = jnp.float32
BF16 = jnp.bfloat16
VMEM_BUDGET = 52 * 2**20
VMEM_LIMIT = 60 * 2**20


def unit_rows(rows):
    scale = lax.rsqrt(jnp.sum(rows * rows, axis=1, keepdims=True) + 1e-06)
    return (rows * scale, scale)


def fold_lanes(block):
    total = block[:, :128]
    for at in range(128, block.shape[1], 128):
        total = total + block[:, at : at + 128]
    return total


def head_kernel(
    nd, npr, tile,
    x_ref, t_ref, w_ref, img_ref, glob_ref, dx_ref, dw_ref,
    wraw, wn, q, e, tt, s2, xb, zacc, a_ref, cs, cvec, dwp, dwa, dwb, dwc, dwf,
    wsend, wrecv, csend, crecv, dsend, drecv,
):
    me_d, me_p = lax.axis_index("dp"), lax.axis_index("proto")
    crops, bot = x_ref.shape
    teach = t_ref.shape[0]
    protos = w_ref.shape[1]
    tiles = crops // tile
    gain = (npr * protos / 64.0) / 0.1
    quarter = bot // nd
    half = bot // 2
    core_d = me_d + 1 - 2 * (me_d % 2)
    far_d = (me_d + nd // 2) % nd
    diag_d = (core_d + nd // 2) % nd
    flip = lambda b: b + 1 - 2 * (b % 2)
    y_p = flip(me_p)
    z_ps = [(me_p + 2 * k) % npr for k in range(1, npr // 2)]

    barrier = pltpu.get_barrier_semaphore()
    peers = [(me_d, p) for p in z_ps + [y_p]] + [(d, me_p) for d in (core_d, far_d, diag_d)]
    for peer in peers:
        pl.semaphore_signal(barrier, inc=1, device_id=peer, device_id_type=MESH)
    pl.semaphore_wait(barrier, len(peers))

    started = []

    def rows_of(which):
        return pl.ds(pl.multiple_of(which * quarter, quarter), quarter)

    def send_w(src, block, which, target):
        copy = pltpu.make_async_remote_copy(
            src_ref=src,
            dst_ref=wraw.at[block, rows_of(which)],
            send_sem=wsend.at[len(started)],
            recv_sem=wrecv.at[block, which],
            device_id=target,
            device_id_type=MESH,
        )
        copy.start()
        started.append(copy)

    def arrived(block, which):
        here = wraw.at[block, rows_of(which)]
        pltpu.make_async_remote_copy(
            src_ref=here, dst_ref=here, send_sem=wsend.at[0], recv_sem=wrecv.at[block, which],
            device_id=(core_d, me_p), device_id_type=MESH,
        ).wait_recv()

    def pass_w(block, which, target):
        send_w(wraw.at[block, rows_of(which)], block, which, target)

    own_part = w_ref.at[rows_of(me_d)]
    for p in z_ps + [y_p]:
        send_w(own_part, me_p, me_d, (me_d, p))

    t_b = unit_rows(t_ref[...].astype(F32))[0].astype(BF16)

    def ready(block, raw):
        w = raw.astype(F32)
        w_b = (w * lax.rsqrt(jnp.sum(w * w, axis=0, keepdims=True) + 1e-06)).astype(BF16)
        wn[block] = w_b
        q_b = jnp.exp2(jnp.dot(t_b, w_b, preferred_element_type=F32) * (LOG2E / 0.07))
        q[block] = q_b
        cs[0, me_d, pl.ds(block, 1), :] = jnp.sum(q_b, axis=0, keepdims=True)

    def student_block(b):
        @pl.loop(0, tiles)
        def _(i):
            rows = pl.ds(pl.multiple_of(i * tile, tile), tile)
            logits = jnp.dot(xb[rows, :], wn[b], preferred_element_type=F32)
            expo = jnp.exp2(logits * (LOG2E / 0.1))
            e[b, rows, :] = expo
            zacc[b, rows, :] = fold_lanes(expo)

    def normalize_students():
        @pl.loop(0, tiles)
        def _(i):
            rows = pl.ds(pl.multiple_of(i * tile, tile), tile)
            xb[rows, :] = unit_rows(x_ref[rows, :].astype(F32))[0].astype(BF16)

    def pick_targets():
        offset = me_d * (teach // GLOBALS)
        image = (img_ref[...].reshape(1, crops) - offset) * GLOBALS
        glob = glob_ref[...].reshape(1, crops)
        width = 256 if crops % 256 == 0 else 128
        for at in range(0, crops, width):
            rows = slice(at, at + width)
            slot = lax.broadcasted_iota(jnp.int32, (teach, width), 0)
            pick = jnp.zeros((teach, width), F32)
            for v in range(GLOBALS):
                here = (slot == image[:, rows] + v) & (glob[:, rows] != v)
                pick = pick + jnp.where(here, 1.0, 0.0)
            pick = jnp.transpose(pick)
            s2[rows, :teach] = pick.astype(BF16)
            s2[rows, teach:] = pick.astype(BF16)
            count = jnp.sum(pick, axis=1, keepdims=True)
            a_ref[rows, :] = jnp.broadcast_to(count, (width, 128))

    order = [y_p] + z_ps + [flip(p) for p in z_ps]

    def relay(at):
        block = order[at]
        arrived(block, me_d)
        if 1 <= at <= len(z_ps):
            pass_w(block, me_d, (me_d, y_p))
        pass_w(block, me_d, (far_d, me_p))
        pass_w(block, me_d, (core_d, me_p))

    def share(at):
        arrived(order[at], far_d)
        pass_w(order[at], far_d, (core_d, me_p))

    def take(at):
        block = order[at]
        arrived(block, core_d)
        arrived(block, diag_d)
        ready(block, wraw[block])

    ready(me_p, w_ref[...])
    count = len(order)
    relay(0)
    normalize_students()
    student_block(me_p)
    for at in range(1, len(z_ps) + 1):
        relay(at)
    pick_targets()
    share(0)
    later = count % ITERS
    for at in range(count):
        if at + len(z_ps) + 1 < count:
            relay(at + len(z_ps) + 1)
        if at + 1 < count:
            share(at + 1)
        take(at)
        if at < later:
            student_block(order[at])

    def row_scale():
        def body(b, acc):
            return acc + fold_lanes(q[b] * cvec[pl.ds(b, 1), :])
        acc = lax.fori_loop(0, npr, body, jnp.zeros((teach, 128), F32))
        return 1.0 / jnp.sum(acc, axis=1, keepdims=True)

    for step in range(ITERS):
        if step:
            r = row_scale()

            @pl.loop(0, npr)
            def _(b):
                cs[step, me_d, pl.ds(b, 1), :] = jnp.sum(q[b] * r, axis=0, keepdims=True)

        copies = []
        for k, d in enumerate((core_d, far_d, diag_d)):
            copy = pltpu.make_async_remote_copy(
                src_ref=cs.at[step, me_d],
                dst_ref=cs.at[step, me_d],
                send_sem=csend.at[step, k],
                recv_sem=crecv.at[step, k],
                device_id=(d, me_p),
                device_id_type=MESH,
            )
            copy.start()
            copies.append(copy)
        for at in range(later + step, count, ITERS):
            student_block(order[at])
        for copy in copies:
            copy.wait()
        total = cs[step, 0]
        for d in range(1, nd):
            total = total + cs[step, d]
        cvec[...] = 1.0 / total
    r = row_scale() * gain

    @pl.loop(0, npr)
    def _(b):
        target = q[b] * r * cvec[pl.ds(b, 1), :]
        high = target.astype(BF16)
        tt[b, :teach, :] = high
        tt[b, teach:, :] = (target - high.astype(F32)).astype(BF16)

    def grad(b, rows):
        target = jnp.dot(s2[rows, :], tt[b], preferred_element_type=F32)
        scale = jnp.concatenate([a_ref[rows, :]] * (protos // 128), axis=1)
        return (e[b, rows, :] * scale - target).astype(BF16)

    dwp[...] = jnp.zeros_like(dwp)

    @pl.loop(0, tiles)
    def _(i):
        rows = pl.ds(pl.multiple_of(i * tile, tile), tile)
        z = zacc[0, rows, :]
        for b in range(1, npr):
            z = z + zacc[b, rows, :]
        a_ref[rows, :] = a_ref[rows, :] * (gain / jnp.sum(z, axis=1, keepdims=True))
        dwp[...] += lax.dot_general(
            xb[rows, :], grad(me_p, rows), (((0,), (0,)), ((), ())), preferred_element_type=F32
        )

    def part(which):
        return pl.ds(pl.multiple_of(which * half, half), half)

    mine, other = me_d % 2, 1 - me_d % 2

    def send_d(k, src, dst, d):
        copy = pltpu.make_async_remote_copy(
            src_ref=src, dst_ref=dst, send_sem=dsend.at[k], recv_sem=drecv.at[k],
            device_id=(d, me_p), device_id_type=MESH,
        )
        copy.start()
        return copy

    def student_sums(first, last):
        @pl.loop(first, last)
        def _(b):
            for i in range(tiles):
                rows = pl.ds(i * tile, tile)
                dx_ref[rows, :] += lax.dot_general(
                    grad(b, rows), wn[b], (((1,), (1,)), ((), ())), preferred_element_type=F32
                )

    first = send_d(0, dwp.at[part(other)], dwa, core_d)
    dx_ref[...] = jnp.zeros_like(dx_ref)
    student_sums(0, npr // 4)
    first.wait()
    dwb[...] = dwp[part(mine), :] + dwa[...]
    second = send_d(1, dwb, dwc, far_d)
    student_sums(npr // 4, npr)
    second.wait()
    dwf[part(mine), :] = dwb[...] + dwc[...]
    third = send_d(2, dwf.at[part(mine)], dwf.at[part(mine)], core_d)

    @pl.loop(0, tiles)
    def _(i):
        rows = pl.ds(pl.multiple_of(i * tile, tile), tile)
        x_n, x_r = unit_rows(x_ref[rows, :].astype(F32))
        dxn = dx_ref[rows, :]
        dx_ref[rows, :] = x_r * (dxn - x_n * jnp.sum(x_n * dxn, axis=1, keepdims=True))

    third.wait()
    w = w_ref[...].astype(F32)
    v_r = lax.rsqrt(jnp.sum(w * w, axis=0, keepdims=True) + 1e-06)
    w_n = w * v_r
    dwn = dwf[...]
    dw_ref[...] = v_r * (dwn - w_n * jnp.sum(w_n * dwn, axis=0, keepdims=True))
    for copy in started:
        copy.wait_send()


def row_tile(crops):
    return next((t for t in (640, 512, 256, 128) if crops % t == 0), 0)


def scratch_of(nd, npr, crops, bot, teach, protos):
    links = nd * (npr - 1)
    return [
        ((npr, bot, protos), BF16),
        ((npr, bot, protos), BF16),
        ((npr, teach, protos), F32),
        ((npr, crops, protos), F32),
        ((npr, 2 * teach, protos), BF16),
        ((crops, 2 * teach), BF16),
        ((crops, bot), BF16),
        ((npr, crops, 128), F32),
        ((crops, 128), F32),
        ((ITERS, nd, npr, protos), F32),
        ((npr, protos), F32),
        ((bot, protos), F32),
        ((bot // 2, protos), F32),
        ((bot // 2, protos), F32),
        ((bot // 2, protos), F32),
        ((bot, protos), F32),
    ], links


def fused(student_rows, teacher_rows, prototypes, crop_image, crop_global):
    nd, npr = lax.axis_size("dp"), lax.axis_size("proto")
    crops, bot = student_rows.shape
    teach, protos = teacher_rows.shape[0], prototypes.shape[1]
    shapes, links = scratch_of(nd, npr, crops, bot, teach, protos)
    whole = pl.BlockSpec(memory_space=pltpu.VMEM)
    return pl.pallas_call(
        functools.partial(head_kernel, nd, npr, row_tile(crops)),
        out_shape=(
            jax.ShapeDtypeStruct((crops, bot), F32),
            jax.ShapeDtypeStruct((bot, protos), F32),
        ),
        in_specs=[whole] * 5,
        out_specs=(whole, whole),
        scratch_shapes=[pltpu.VMEM(shape, kind) for shape, kind in shapes]
        + [
            pltpu.SemaphoreType.DMA((links,)),
            pltpu.SemaphoreType.DMA((npr, nd)),
            pltpu.SemaphoreType.DMA((ITERS, nd - 1)),
            pltpu.SemaphoreType.DMA((ITERS, nd - 1)),
            pltpu.SemaphoreType.DMA((3,)),
            pltpu.SemaphoreType.DMA((3,)),
        ],
        compiler_params=pltpu.CompilerParams(
            collective_id=0, has_side_effects=True, vmem_limit_bytes=VMEM_LIMIT
        ),
        cost_estimate=pl.CostEstimate(
            flops=10 * crops * npr * protos * bot,
            bytes_accessed=4 * (crops * bot + bot * protos),
            transcendentals=npr * protos * (crops + teach),
        ),
    )(student_rows, teacher_rows, prototypes, crop_image, crop_global)


def fits(nd, npr, crops, bot, teach, protos):
    shapes, _ = scratch_of(nd, npr, crops, bot, teach, protos)
    size = 0
    for shape, kind in shapes:
        count = 1
        for extent in shape:
            count *= extent
        size += count * jnp.dtype(kind).itemsize
    tiled = row_tile(crops) and protos % 128 == 0 and bot % (nd * 16) == 0 and teach % 128 == 0
    return nd == 4 and npr % 2 == 0 and npr > ITERS and bool(tiled) and size <= VMEM_BUDGET


def on_device(student_rows, teacher_rows, prototypes, crop_image, crop_global):
    sizes = (*student_rows.shape, teacher_rows.shape[0], prototypes.shape[1])
    if fits(lax.axis_size("dp"), lax.axis_size("proto"), *sizes):
        return fused(student_rows, teacher_rows, prototypes, crop_image, crop_global)
    total_protos = lax.axis_size("proto") * prototypes.shape[1]
    img_local = teacher_rows.shape[0] // GLOBALS
    teach_total = lax.axis_size("dp") * teacher_rows.shape[0]
    weights = prototypes.astype(jnp.float32)
    col_scale = lax.rsqrt(jnp.sum(weights * weights, axis=0, keepdims=True) + 1e-06)
    w_norm = weights * col_scale
    w_bf = w_norm.astype(jnp.bfloat16)
    t_norm, t_scale = unit_rows(teacher_rows.astype(jnp.float32))
    t_bf = t_norm.astype(jnp.bfloat16)
    q_mat = jnp.exp(jnp.dot(t_bf, w_bf, preferred_element_type=jnp.float32) / 0.07)
    for step in range(ITERS):
        q_mat = q_mat / lax.psum(jnp.sum(q_mat, axis=0), "dp")[None, :] / total_protos
        row_tot = lax.psum(jnp.sum(q_mat, axis=1), "proto")
        q_mat = q_mat / row_tot[:, None] / teach_total
    targets = q_mat * teach_total
    x_norm, x_scale = unit_rows(student_rows.astype(jnp.float32))
    x_bf = x_norm.astype(jnp.bfloat16)
    logits = jnp.dot(x_bf, w_bf, preferred_element_type=jnp.float32) / 0.1
    expo = jnp.exp(logits)
    total = lax.psum(jnp.sum(expo, axis=1), "proto")
    probs = expo / total[:, None]
    image_here = crop_image - lax.axis_index("dp") * img_local
    first = jnp.take(targets, GLOBALS * image_here, axis=0)
    second = jnp.take(targets, GLOBALS * image_here + 1, axis=0)
    keep_first = (crop_global != 0).astype(jnp.float32)[:, None]
    keep_second = (crop_global != 1).astype(jnp.float32)[:, None]
    target_rows = first * keep_first + second * keep_second
    count = keep_first + keep_second
    scale_out = total_protos / 64.0
    grad_bf = (scale_out * (count * probs - target_rows) / 0.1).astype(jnp.bfloat16)
    crops_here = grad_bf.shape[0]
    groups = lax.axis_size("proto")
    share = -(-crops_here // groups)
    dxn_share = lax.psum_scatter(
        lax.dot_general(
            grad_bf, w_bf, (((1,), (1,)), ((), ())), preferred_element_type=jnp.float32
        ),
        "proto",
        scatter_dimension=0,
        tiled=True,
    )
    begin = lax.axis_index("proto") * share
    xn_share = lax.dynamic_slice_in_dim(x_norm, begin, share, 0)
    xr_share = lax.dynamic_slice_in_dim(x_scale, begin, share, 0)
    dx_share = xr_share * (
        dxn_share - xn_share * jnp.sum(xn_share * dxn_share, axis=1, keepdims=True)
    )
    student_grad = lax.all_gather(dx_share, "proto", axis=0, tiled=True)
    dwn_local = lax.dot_general(
        x_bf, grad_bf, (((0,), (0,)), ((), ())), preferred_element_type=jnp.float32
    )
    dwn_total = lax.psum(dwn_local, "dp")
    proto_grad = col_scale * (
        dwn_total - w_norm * jnp.sum(w_norm * dwn_total, axis=0, keepdims=True)
    )
    return (student_grad, proto_grad)


def solution(mesh):
    placed = (P("dp", None), P("dp", None), P(None, "proto"), P("dp"), P("dp"))
    return jax.shard_map(
        on_device,
        mesh=mesh,
        in_specs=placed,
        out_specs=(P("dp", None), P(None, "proto")),
        check_vma=False,
    )
```

```python
import functools
import math

import jax
import jax.numpy as jnp
from jax import lax
from jax.experimental import pallas as pl
from jax.experimental.pallas import tpu as pltpu
from jax.sharding import PartitionSpec as P

GLOBALS = 2
ITERS = 3
LOG2E = math.log2(math.e)
MESH = pl.DeviceIdType.MESH
F32 = jnp.float32
BF16 = jnp.bfloat16
VMEM_BUDGET = 52 * 2**20
VMEM_LIMIT = 60 * 2**20


def unit_rows(rows):
    scale = lax.rsqrt(jnp.sum(rows * rows, axis=1, keepdims=True) + 1e-06)
    return (rows * scale, scale)


def fold_lanes(block):
    total = block[:, :128]
    for at in range(128, block.shape[1], 128):
        total = total + block[:, at : at + 128]
    return total


def head_kernel(
    nd, npr, tile,
    x_ref, t_ref, w_ref, img_ref, glob_ref, dx_ref, dw_ref,
    wraw, wn, q, e, tt, s2, xb, zacc, a_ref, cs, cvec, dwp, dwa, dwb, dwc, dwf,
    wsend, wrecv, csend, crecv, dsend, drecv,
):
    me_d, me_p = lax.axis_index("dp"), lax.axis_index("proto")
    crops, bot = x_ref.shape
    teach = t_ref.shape[0]
    protos = w_ref.shape[1]
    tiles = crops // tile
    gain = (npr * protos / 64.0) / 0.1
    half = bot // 2
    edge = (half * 3 // 8) // 16 * 16
    reach = half - edge
    core_d = me_d + 1 - 2 * (me_d % 2)
    far_d = (me_d + nd // 2) % nd
    diag_d = (core_d + nd // 2) % nd
    flip = lambda b: b + 1 - 2 * (b % 2)
    y_p = flip(me_p)
    z_ps = [(me_p + 2 * k) % npr for k in range(1, npr // 2)]

    barrier = pltpu.get_barrier_semaphore()
    peers = [(me_d, p) for p in z_ps + [y_p]] + [(d, me_p) for d in (core_d, far_d, diag_d)]
    for peer in peers:
        pl.semaphore_signal(barrier, inc=1, device_id=peer, device_id_type=MESH)
    pl.semaphore_wait(barrier, len(peers))

    started = []

    def fetched(d):
        return pl.ds(pl.multiple_of(d % 2 * half + d // 2 * edge, 16), reach)

    def lent(d):
        return pl.ds(pl.multiple_of(d % 2 * half + d // 2 * reach, 16), edge)

    def send_w(src, block, rows, which, target):
        copy = pltpu.make_async_remote_copy(
            src_ref=src,
            dst_ref=wraw.at[block, rows],
            send_sem=wsend.at[len(started)],
            recv_sem=wrecv.at[block, which],
            device_id=target,
            device_id_type=MESH,
        )
        copy.start()
        started.append(copy)

    def arrived(block, rows, which):
        here = wraw.at[block, rows]
        pltpu.make_async_remote_copy(
            src_ref=here, dst_ref=here, send_sem=wsend.at[0], recv_sem=wrecv.at[block, which],
            device_id=(core_d, me_p), device_id_type=MESH,
        ).wait_recv()

    def pass_w(block, rows, which, target):
        send_w(wraw.at[block, rows], block, rows, which, target)

    for p in z_ps + [y_p]:
        send_w(w_ref.at[fetched(me_d)], me_p, fetched(me_d), me_d, (me_d, p))

    t_b = unit_rows(t_ref[...].astype(F32))[0].astype(BF16)

    def ready(block, raw):
        w = raw.astype(F32)
        w_b = (w * lax.rsqrt(jnp.sum(w * w, axis=0, keepdims=True) + 1e-06)).astype(BF16)
        wn[block] = w_b
        q_b = jnp.exp2(jnp.dot(t_b, w_b, preferred_element_type=F32) * (LOG2E / 0.07))
        q[block] = q_b
        cs[0, me_d, pl.ds(block, 1), :] = jnp.sum(q_b, axis=0, keepdims=True)

    def student_block(b):
        @pl.loop(0, tiles)
        def _(i):
            rows = pl.ds(pl.multiple_of(i * tile, tile), tile)
            logits = jnp.dot(xb[rows, :], wn[b], preferred_element_type=F32)
            expo = jnp.exp2(logits * (LOG2E / 0.1))
            e[b, rows, :] = expo
            zacc[b, rows, :] = fold_lanes(expo)

    def normalize_students():
        @pl.loop(0, tiles)
        def _(i):
            rows = pl.ds(pl.multiple_of(i * tile, tile), tile)
            xb[rows, :] = unit_rows(x_ref[rows, :].astype(F32))[0].astype(BF16)

    def pick_targets():
        offset = me_d * (teach // GLOBALS)
        image = (img_ref[...].reshape(1, crops) - offset) * GLOBALS
        glob = glob_ref[...].reshape(1, crops)
        width = 256 if crops % 256 == 0 else 128
        for at in range(0, crops, width):
            rows = slice(at, at + width)
            slot = lax.broadcasted_iota(jnp.int32, (teach, width), 0)
            pick = jnp.zeros((teach, width), F32)
            for v in range(GLOBALS):
                here = (slot == image[:, rows] + v) & (glob[:, rows] != v)
                pick = pick + jnp.where(here, 1.0, 0.0)
            pick = jnp.transpose(pick)
            s2[rows, :teach] = pick.astype(BF16)
            s2[rows, teach:] = pick.astype(BF16)
            count = jnp.sum(pick, axis=1, keepdims=True)
            a_ref[rows, :] = jnp.broadcast_to(count, (width, 128))

    order = [y_p] + z_ps + [flip(p) for p in z_ps]

    def relay(at):
        block = order[at]
        arrived(block, fetched(me_d), me_d)
        if 1 <= at <= len(z_ps):
            pass_w(block, fetched(me_d), me_d, (me_d, y_p))
        pass_w(block, lent(me_d), me_d, (far_d, me_p))
        pass_w(block, fetched(me_d), me_d, (core_d, me_p))

    def share(at):
        arrived(order[at], lent(far_d), far_d)
        pass_w(order[at], lent(far_d), far_d, (core_d, me_p))

    def take(at):
        block = order[at]
        arrived(block, fetched(core_d), core_d)
        arrived(block, lent(diag_d), diag_d)
        ready(block, wraw[block])

    ready(me_p, w_ref[...])
    count = len(order)
    relay(0)
    normalize_students()
    student_block(me_p)
    for at in range(1, len(z_ps) + 1):
        relay(at)
    pick_targets()
    share(0)
    later = count % ITERS
    for at in range(count):
        if at + len(z_ps) + 1 < count:
            relay(at + len(z_ps) + 1)
        if at + 1 < count:
            share(at + 1)
        take(at)
        if at < later:
            student_block(order[at])

    def row_scale():
        def body(b, acc):
            return acc + fold_lanes(q[b] * cvec[pl.ds(b, 1), :])
        acc = lax.fori_loop(0, npr, body, jnp.zeros((teach, 128), F32))
        return 1.0 / jnp.sum(acc, axis=1, keepdims=True)

    for step in range(ITERS):
        if step:
            r = row_scale()

            @pl.loop(0, npr)
            def _(b):
                cs[step, me_d, pl.ds(b, 1), :] = jnp.sum(q[b] * r, axis=0, keepdims=True)

        copies = []
        for k, d in enumerate((core_d, far_d, diag_d)):
            copy = pltpu.make_async_remote_copy(
                src_ref=cs.at[step, me_d],
                dst_ref=cs.at[step, me_d],
                send_sem=csend.at[step, k],
                recv_sem=crecv.at[step, k],
                device_id=(d, me_p),
                device_id_type=MESH,
            )
            copy.start()
            copies.append(copy)
        for at in range(later + step, count, ITERS):
            student_block(order[at])
        for copy in copies:
            copy.wait()
        total = cs[step, 0]
        for d in range(1, nd):
            total = total + cs[step, d]
        cvec[...] = 1.0 / total
    r = row_scale() * gain

    @pl.loop(0, npr)
    def _(b):
        target = q[b] * r * cvec[pl.ds(b, 1), :]
        high = target.astype(BF16)
        tt[b, :teach, :] = high
        tt[b, teach:, :] = (target - high.astype(F32)).astype(BF16)

    def grad(b, rows):
        target = jnp.dot(s2[rows, :], tt[b], preferred_element_type=F32)
        scale = jnp.concatenate([a_ref[rows, :]] * (protos // 128), axis=1)
        return (e[b, rows, :] * scale - target).astype(BF16)

    dwp[...] = jnp.zeros_like(dwp)

    @pl.loop(0, tiles)
    def _(i):
        rows = pl.ds(pl.multiple_of(i * tile, tile), tile)
        z = zacc[0, rows, :]
        for b in range(1, npr):
            z = z + zacc[b, rows, :]
        a_ref[rows, :] = a_ref[rows, :] * (gain / jnp.sum(z, axis=1, keepdims=True))
        dwp[...] += lax.dot_general(
            xb[rows, :], grad(me_p, rows), (((0,), (0,)), ((), ())), preferred_element_type=F32
        )

    def part(which):
        return pl.ds(pl.multiple_of(which * half, half), half)

    mine, other = me_d % 2, 1 - me_d % 2

    def send_d(k, src, dst, d):
        copy = pltpu.make_async_remote_copy(
            src_ref=src, dst_ref=dst, send_sem=dsend.at[k], recv_sem=drecv.at[k],
            device_id=(d, me_p), device_id_type=MESH,
        )
        copy.start()
        return copy

    def student_sums(first, last):
        @pl.loop(first, last)
        def _(b):
            for i in range(tiles):
                rows = pl.ds(i * tile, tile)
                dx_ref[rows, :] += lax.dot_general(
                    grad(b, rows), wn[b], (((1,), (1,)), ((), ())), preferred_element_type=F32
                )

    first = send_d(0, dwp.at[part(other)], dwa, core_d)
    dx_ref[...] = jnp.zeros_like(dx_ref)
    student_sums(0, npr // 4)
    first.wait()
    dwb[...] = dwp[part(mine), :] + dwa[...]
    second = send_d(1, dwb, dwc, far_d)
    student_sums(npr // 4, npr)
    second.wait()
    dwf[part(mine), :] = dwb[...] + dwc[...]
    third = send_d(2, dwf.at[part(mine)], dwf.at[part(mine)], core_d)
    third.wait()
    dw_ref[...] = dwf[...]
    for copy in started:
        copy.wait_send()


def project_kernel(x_ref, w_ref, dxn_ref, dwn_ref, dx_ref, dw_ref):
    x_n, x_r = unit_rows(x_ref[...].astype(F32))
    dxn = dxn_ref[...]
    dx_ref[...] = x_r * (dxn - x_n * jnp.sum(x_n * dxn, axis=1, keepdims=True))
    w = w_ref[...].astype(F32)
    v_r = lax.rsqrt(jnp.sum(w * w, axis=0, keepdims=True) + 1e-06)
    w_n = w * v_r
    dwn = dwn_ref[...]
    dw_ref[...] = v_r * (dwn - w_n * jnp.sum(w_n * dwn, axis=0, keepdims=True))


def project(student_rows, prototypes, dxn, dwn):
    crops, bot = student_rows.shape
    protos = prototypes.shape[1]
    steps = protos // 128
    if crops % (16 * steps):
        steps = 1
    rows = pl.BlockSpec((crops // steps, bot), lambda i: (i, 0))
    columns = pl.BlockSpec((bot, protos // steps), lambda i: (0, i))
    return pl.pallas_call(
        project_kernel,
        grid=(steps,),
        out_shape=(jax.ShapeDtypeStruct(dxn.shape, F32), jax.ShapeDtypeStruct(dwn.shape, F32)),
        in_specs=[rows, columns, rows, columns],
        out_specs=(rows, columns),
    )(student_rows, prototypes, dxn, dwn)


def row_tile(crops):
    return next((t for t in (640, 512, 256, 128) if crops % t == 0), 0)


def scratch_of(nd, npr, crops, bot, teach, protos):
    links = nd * (npr - 1)
    return [
        ((npr, bot, protos), BF16),
        ((npr, bot, protos), BF16),
        ((npr, teach, protos), F32),
        ((npr, crops, protos), F32),
        ((npr, 2 * teach, protos), BF16),
        ((crops, 2 * teach), BF16),
        ((crops, bot), BF16),
        ((npr, crops, 128), F32),
        ((crops, 128), F32),
        ((ITERS, nd, npr, protos), F32),
        ((npr, protos), F32),
        ((bot, protos), F32),
        ((bot // 2, protos), F32),
        ((bot // 2, protos), F32),
        ((bot // 2, protos), F32),
        ((bot, protos), F32),
    ], links


def fused(student_rows, teacher_rows, prototypes, crop_image, crop_global):
    nd, npr = lax.axis_size("dp"), lax.axis_size("proto")
    crops, bot = student_rows.shape
    teach, protos = teacher_rows.shape[0], prototypes.shape[1]
    shapes, links = scratch_of(nd, npr, crops, bot, teach, protos)
    whole = pl.BlockSpec(memory_space=pltpu.VMEM)
    dxn, dwn = pl.pallas_call(
        functools.partial(head_kernel, nd, npr, row_tile(crops)),
        out_shape=(
            jax.ShapeDtypeStruct((crops, bot), F32),
            jax.ShapeDtypeStruct((bot, protos), F32),
        ),
        in_specs=[whole] * 5,
        out_specs=(whole, whole),
        scratch_shapes=[pltpu.VMEM(shape, kind) for shape, kind in shapes]
        + [
            pltpu.SemaphoreType.DMA((links,)),
            pltpu.SemaphoreType.DMA((npr, nd)),
            pltpu.SemaphoreType.DMA((ITERS, nd - 1)),
            pltpu.SemaphoreType.DMA((ITERS, nd - 1)),
            pltpu.SemaphoreType.DMA((3,)),
            pltpu.SemaphoreType.DMA((3,)),
        ],
        compiler_params=pltpu.CompilerParams(
            collective_id=0, has_side_effects=True, vmem_limit_bytes=VMEM_LIMIT
        ),
        cost_estimate=pl.CostEstimate(
            flops=10 * crops * npr * protos * bot,
            bytes_accessed=4 * (crops * bot + bot * protos),
            transcendentals=npr * protos * (crops + teach),
        ),
    )(student_rows, teacher_rows, prototypes, crop_image, crop_global)
    return project(student_rows, prototypes, dxn, dwn)


def fits(nd, npr, crops, bot, teach, protos):
    shapes, _ = scratch_of(nd, npr, crops, bot, teach, protos)
    size = 0
    for shape, kind in shapes:
        count = 1
        for extent in shape:
            count *= extent
        size += count * jnp.dtype(kind).itemsize
    tiled = row_tile(crops) and protos % 128 == 0 and bot % 128 == 0 and teach % 128 == 0
    return nd == 4 and npr % 2 == 0 and npr > ITERS and bool(tiled) and size <= VMEM_BUDGET


def on_device(student_rows, teacher_rows, prototypes, crop_image, crop_global):
    sizes = (*student_rows.shape, teacher_rows.shape[0], prototypes.shape[1])
    if fits(lax.axis_size("dp"), lax.axis_size("proto"), *sizes):
        return fused(student_rows, teacher_rows, prototypes, crop_image, crop_global)
    total_protos = lax.axis_size("proto") * prototypes.shape[1]
    img_local = teacher_rows.shape[0] // GLOBALS
    teach_total = lax.axis_size("dp") * teacher_rows.shape[0]
    weights = prototypes.astype(jnp.float32)
    col_scale = lax.rsqrt(jnp.sum(weights * weights, axis=0, keepdims=True) + 1e-06)
    w_norm = weights * col_scale
    w_bf = w_norm.astype(jnp.bfloat16)
    t_norm, t_scale = unit_rows(teacher_rows.astype(jnp.float32))
    t_bf = t_norm.astype(jnp.bfloat16)
    q_mat = jnp.exp(jnp.dot(t_bf, w_bf, preferred_element_type=jnp.float32) / 0.07)
    for step in range(ITERS):
        q_mat = q_mat / lax.psum(jnp.sum(q_mat, axis=0), "dp")[None, :] / total_protos
        row_tot = lax.psum(jnp.sum(q_mat, axis=1), "proto")
        q_mat = q_mat / row_tot[:, None] / teach_total
    targets = q_mat * teach_total
    x_norm, x_scale = unit_rows(student_rows.astype(jnp.float32))
    x_bf = x_norm.astype(jnp.bfloat16)
    logits = jnp.dot(x_bf, w_bf, preferred_element_type=jnp.float32) / 0.1
    expo = jnp.exp(logits)
    total = lax.psum(jnp.sum(expo, axis=1), "proto")
    probs = expo / total[:, None]
    image_here = crop_image - lax.axis_index("dp") * img_local
    first = jnp.take(targets, GLOBALS * image_here, axis=0)
    second = jnp.take(targets, GLOBALS * image_here + 1, axis=0)
    keep_first = (crop_global != 0).astype(jnp.float32)[:, None]
    keep_second = (crop_global != 1).astype(jnp.float32)[:, None]
    target_rows = first * keep_first + second * keep_second
    count = keep_first + keep_second
    scale_out = total_protos / 64.0
    grad_bf = (scale_out * (count * probs - target_rows) / 0.1).astype(jnp.bfloat16)
    crops_here = grad_bf.shape[0]
    groups = lax.axis_size("proto")
    share = -(-crops_here // groups)
    dxn_share = lax.psum_scatter(
        lax.dot_general(
            grad_bf, w_bf, (((1,), (1,)), ((), ())), preferred_element_type=jnp.float32
        ),
        "proto",
        scatter_dimension=0,
        tiled=True,
    )
    begin = lax.axis_index("proto") * share
    xn_share = lax.dynamic_slice_in_dim(x_norm, begin, share, 0)
    xr_share = lax.dynamic_slice_in_dim(x_scale, begin, share, 0)
    dx_share = xr_share * (
        dxn_share - xn_share * jnp.sum(xn_share * dxn_share, axis=1, keepdims=True)
    )
    student_grad = lax.all_gather(dx_share, "proto", axis=0, tiled=True)
    dwn_local = lax.dot_general(
        x_bf, grad_bf, (((0,), (0,)), ((), ())), preferred_element_type=jnp.float32
    )
    dwn_total = lax.psum(dwn_local, "dp")
    proto_grad = col_scale * (
        dwn_total - w_norm * jnp.sum(w_norm * dwn_total, axis=0, keepdims=True)
    )
    return (student_grad, proto_grad)


def solution(mesh):
    placed = (P("dp", None), P("dp", None), P(None, "proto"), P("dp"), P("dp"))
    return jax.shard_map(
        on_device,
        mesh=mesh,
        in_specs=placed,
        out_specs=(P("dp", None), P(None, "proto")),
        check_vma=False,
    )
```

```python
import functools
import math

import jax
import jax.numpy as jnp
from jax import lax
from jax.experimental import pallas as pl
from jax.experimental.pallas import tpu as pltpu
from jax.sharding import PartitionSpec as P

GLOBALS = 2
ITERS = 3
LOG2E = math.log2(math.e)
MESH = pl.DeviceIdType.MESH
F32 = jnp.float32
BF16 = jnp.bfloat16
VMEM_BUDGET = 52 * 2**20
VMEM_LIMIT = 60 * 2**20


def unit_rows(rows):
    scale = lax.rsqrt(jnp.sum(rows * rows, axis=1, keepdims=True) + 1e-06)
    return (rows * scale, scale)


def fold_lanes(block):
    total = block[:, :128]
    for at in range(128, block.shape[1], 128):
        total = total + block[:, at : at + 128]
    return total


def head_kernel(
    nd, npr, tile,
    x_ref, t_ref, w_ref, img_ref, glob_ref, dx_ref, dw_ref,
    wraw, wn, q, e, tt, s2, xb, zacc, a_ref, cs, cvec, dwp, dwa, dwb, dwc, dwf,
    wsend, wrecv, csend, crecv, dsend, drecv,
):
    me_d, me_p = lax.axis_index("dp"), lax.axis_index("proto")
    crops, bot = x_ref.shape
    teach = t_ref.shape[0]
    protos = w_ref.shape[1]
    tiles = crops // tile
    gain = (npr * protos / 64.0) / 0.1
    quarter = bot // nd
    half = bot // 2
    core_d = me_d + 1 - 2 * (me_d % 2)
    far_d = (me_d + nd // 2) % nd
    diag_d = (core_d + nd // 2) % nd
    flip = lambda b: b + 1 - 2 * (b % 2)
    y_p = flip(me_p)
    z_ps = [(me_p + 2 * k) % npr for k in range(1, npr // 2)]

    barrier = pltpu.get_barrier_semaphore()
    peers = [(me_d, p) for p in z_ps + [y_p]] + [(d, me_p) for d in (core_d, far_d, diag_d)]
    for peer in peers:
        pl.semaphore_signal(barrier, inc=1, device_id=peer, device_id_type=MESH)
    pl.semaphore_wait(barrier, len(peers))

    started = []

    def rows_of(which):
        return pl.ds(pl.multiple_of(which * quarter, quarter), quarter)

    def send_w(src, block, which, target):
        copy = pltpu.make_async_remote_copy(
            src_ref=src,
            dst_ref=wraw.at[block, rows_of(which)],
            send_sem=wsend.at[len(started)],
            recv_sem=wrecv.at[block, which],
            device_id=target,
            device_id_type=MESH,
        )
        copy.start()
        started.append(copy)

    def arrived(block, which):
        here = wraw.at[block, rows_of(which)]
        pltpu.make_async_remote_copy(
            src_ref=here, dst_ref=here, send_sem=wsend.at[0], recv_sem=wrecv.at[block, which],
            device_id=(core_d, me_p), device_id_type=MESH,
        ).wait_recv()

    def pass_w(block, which, target):
        send_w(wraw.at[block, rows_of(which)], block, which, target)

    own_part = w_ref.at[rows_of(me_d)]
    for p in z_ps + [y_p]:
        send_w(own_part, me_p, me_d, (me_d, p))

    t_b = unit_rows(t_ref[...].astype(F32))[0].astype(BF16)

    def ready(block, raw):
        w = raw.astype(F32)
        w_b = (w * lax.rsqrt(jnp.sum(w * w, axis=0, keepdims=True) + 1e-06)).astype(BF16)
        wn[block] = w_b
        q_b = jnp.exp2(jnp.dot(t_b, w_b, preferred_element_type=F32) * (LOG2E / 0.07))
        q[block] = q_b
        cs[0, me_d, pl.ds(block, 1), :] = jnp.sum(q_b, axis=0, keepdims=True)

    def student_block(b):
        for i in range(tiles):
            rows = pl.ds(i * tile, tile)
            logits = jnp.dot(xb[rows, :], wn[b], preferred_element_type=F32)
            expo = jnp.exp2(logits * (LOG2E / 0.1))
            e[b, rows, :] = expo
            zacc[b, rows, :] = fold_lanes(expo)

    def normalize_students():
        @pl.loop(0, tiles)
        def _(i):
            rows = pl.ds(pl.multiple_of(i * tile, tile), tile)
            xb[rows, :] = unit_rows(x_ref[rows, :].astype(F32))[0].astype(BF16)

    def pick_targets():
        offset = me_d * (teach // GLOBALS)
        image = (img_ref[...].reshape(1, crops) - offset) * GLOBALS
        glob = glob_ref[...].reshape(1, crops)
        width = 256 if crops % 256 == 0 else 128
        for at in range(0, crops, width):
            rows = slice(at, at + width)
            slot = lax.broadcasted_iota(jnp.int32, (teach, width), 0)
            pick = jnp.zeros((teach, width), F32)
            for v in range(GLOBALS):
                here = (slot == image[:, rows] + v) & (glob[:, rows] != v)
                pick = pick + jnp.where(here, 1.0, 0.0)
            pick = jnp.transpose(pick)
            s2[rows, :teach] = pick.astype(BF16)
            s2[rows, teach:] = pick.astype(BF16)
            count = jnp.sum(pick, axis=1, keepdims=True)
            a_ref[rows, :] = jnp.broadcast_to(count, (width, 128))

    order = [y_p] + z_ps + [flip(p) for p in z_ps]

    def relay(at):
        block = order[at]
        arrived(block, me_d)
        if 1 <= at <= len(z_ps):
            pass_w(block, me_d, (me_d, y_p))
        pass_w(block, me_d, (far_d, me_p))
        pass_w(block, me_d, (core_d, me_p))

    def share(at):
        arrived(order[at], far_d)
        pass_w(order[at], far_d, (core_d, me_p))

    def take(at):
        block = order[at]
        arrived(block, core_d)
        arrived(block, diag_d)
        ready(block, wraw[block])

    ready(me_p, w_ref[...])
    count = len(order)
    relay(0)
    normalize_students()
    student_block(me_p)
    for at in range(1, len(z_ps) + 1):
        relay(at)
    pick_targets()
    share(0)
    later = count % ITERS
    for at in range(count):
        if at + len(z_ps) + 1 < count:
            relay(at + len(z_ps) + 1)
        if at + 1 < count:
            share(at + 1)
        take(at)
        if at < later:
            student_block(order[at])

    def row_scale():
        acc = jnp.zeros((teach, 128), F32)
        for b in range(npr):
            acc = acc + fold_lanes(q[b] * cvec[b : b + 1, :])
        return 1.0 / jnp.sum(acc, axis=1, keepdims=True)

    for step in range(ITERS):
        if step:
            r = row_scale()

            for b in range(npr):
                cs[step, me_d, b : b + 1, :] = jnp.sum(q[b] * r, axis=0, keepdims=True)

        copies = []
        for k, d in enumerate((core_d, far_d, diag_d)):
            copy = pltpu.make_async_remote_copy(
                src_ref=cs.at[step, me_d],
                dst_ref=cs.at[step, me_d],
                send_sem=csend.at[step, k],
                recv_sem=crecv.at[step, k],
                device_id=(d, me_p),
                device_id_type=MESH,
            )
            copy.start()
            copies.append(copy)
        for at in range(later + step, count, ITERS):
            student_block(order[at])
        for copy in copies:
            copy.wait()
        total = cs[step, 0]
        for d in range(1, nd):
            total = total + cs[step, d]
        cvec[...] = 1.0 / total
    r = row_scale() * gain

    for b in range(npr):
        target = q[b] * r * cvec[b : b + 1, :]
        high = target.astype(BF16)
        tt[b, :teach, :] = high
        tt[b, teach:, :] = (target - high.astype(F32)).astype(BF16)

    def grad(b, rows):
        target = jnp.dot(s2[rows, :], tt[b], preferred_element_type=F32)
        scale = jnp.concatenate([a_ref[rows, :]] * (protos // 128), axis=1)
        return (e[b, rows, :] * scale - target).astype(BF16)

    dwp[...] = jnp.zeros_like(dwp)

    @pl.loop(0, tiles)
    def _(i):
        rows = pl.ds(pl.multiple_of(i * tile, tile), tile)
        z = zacc[0, rows, :]
        for b in range(1, npr):
            z = z + zacc[b, rows, :]
        a_ref[rows, :] = a_ref[rows, :] * (gain / jnp.sum(z, axis=1, keepdims=True))
        dwp[...] += lax.dot_general(
            xb[rows, :], grad(me_p, rows), (((0,), (0,)), ((), ())), preferred_element_type=F32
        )

    def part(which):
        return pl.ds(pl.multiple_of(which * half, half), half)

    mine, other = me_d % 2, 1 - me_d % 2

    def send_d(k, src, dst, d):
        copy = pltpu.make_async_remote_copy(
            src_ref=src, dst_ref=dst, send_sem=dsend.at[k], recv_sem=drecv.at[k],
            device_id=(d, me_p), device_id_type=MESH,
        )
        copy.start()
        return copy

    def student_sums(first, last):
        @pl.loop(first, last)
        def _(b):
            for i in range(tiles):
                rows = pl.ds(i * tile, tile)
                dx_ref[rows, :] += lax.dot_general(
                    grad(b, rows), wn[b], (((1,), (1,)), ((), ())), preferred_element_type=F32
                )

    first = send_d(0, dwp.at[part(other)], dwa, core_d)
    dx_ref[...] = jnp.zeros_like(dx_ref)
    student_sums(0, npr // 4)
    first.wait()
    dwb[...] = dwp[part(mine), :] + dwa[...]
    second = send_d(1, dwb, dwc, far_d)
    student_sums(npr // 4, npr)
    second.wait()
    dwf[part(mine), :] = dwb[...] + dwc[...]
    third = send_d(2, dwf.at[part(mine)], dwf.at[part(mine)], core_d)

    @pl.loop(0, tiles)
    def _(i):
        rows = pl.ds(pl.multiple_of(i * tile, tile), tile)
        x_n, x_r = unit_rows(x_ref[rows, :].astype(F32))
        dxn = dx_ref[rows, :]
        dx_ref[rows, :] = x_r * (dxn - x_n * jnp.sum(x_n * dxn, axis=1, keepdims=True))

    third.wait()
    w = w_ref[...].astype(F32)
    v_r = lax.rsqrt(jnp.sum(w * w, axis=0, keepdims=True) + 1e-06)
    w_n = w * v_r
    dwn = dwf[...]
    dw_ref[...] = v_r * (dwn - w_n * jnp.sum(w_n * dwn, axis=0, keepdims=True))
    for copy in started:
        copy.wait_send()


def row_tile(crops):
    return next((t for t in (640, 512, 256, 128) if crops % t == 0), 0)


def scratch_of(nd, npr, crops, bot, teach, protos):
    links = nd * (npr - 1)
    return [
        ((npr, bot, protos), BF16),
        ((npr, bot, protos), BF16),
        ((npr, teach, protos), F32),
        ((npr, crops, protos), F32),
        ((npr, 2 * teach, protos), BF16),
        ((crops, 2 * teach), BF16),
        ((crops, bot), BF16),
        ((npr, crops, 128), F32),
        ((crops, 128), F32),
        ((ITERS, nd, npr, protos), F32),
        ((npr, protos), F32),
        ((bot, protos), F32),
        ((bot // 2, protos), F32),
        ((bot // 2, protos), F32),
        ((bot // 2, protos), F32),
        ((bot, protos), F32),
    ], links


def fused(student_rows, teacher_rows, prototypes, crop_image, crop_global):
    nd, npr = lax.axis_size("dp"), lax.axis_size("proto")
    crops, bot = student_rows.shape
    teach, protos = teacher_rows.shape[0], prototypes.shape[1]
    shapes, links = scratch_of(nd, npr, crops, bot, teach, protos)
    whole = pl.BlockSpec(memory_space=pltpu.VMEM)
    return pl.pallas_call(
        functools.partial(head_kernel, nd, npr, row_tile(crops)),
        out_shape=(
            jax.ShapeDtypeStruct((crops, bot), F32),
            jax.ShapeDtypeStruct((bot, protos), F32),
        ),
        in_specs=[whole] * 5,
        out_specs=(whole, whole),
        scratch_shapes=[pltpu.VMEM(shape, kind) for shape, kind in shapes]
        + [
            pltpu.SemaphoreType.DMA((links,)),
            pltpu.SemaphoreType.DMA((npr, nd)),
            pltpu.SemaphoreType.DMA((ITERS, nd - 1)),
            pltpu.SemaphoreType.DMA((ITERS, nd - 1)),
            pltpu.SemaphoreType.DMA((3,)),
            pltpu.SemaphoreType.DMA((3,)),
        ],
        compiler_params=pltpu.CompilerParams(
            collective_id=0, has_side_effects=True, vmem_limit_bytes=VMEM_LIMIT
        ),
        cost_estimate=pl.CostEstimate(
            flops=10 * crops * npr * protos * bot,
            bytes_accessed=4 * (crops * bot + bot * protos),
            transcendentals=npr * protos * (crops + teach),
        ),
    )(student_rows, teacher_rows, prototypes, crop_image, crop_global)


def fits(nd, npr, crops, bot, teach, protos):
    shapes, _ = scratch_of(nd, npr, crops, bot, teach, protos)
    size = 0
    for shape, kind in shapes:
        count = 1
        for extent in shape:
            count *= extent
        size += count * jnp.dtype(kind).itemsize
    tiled = row_tile(crops) and protos % 128 == 0 and bot % (nd * 16) == 0 and teach % 128 == 0
    return nd == 4 and npr % 2 == 0 and npr > ITERS and bool(tiled) and size <= VMEM_BUDGET


def on_device(student_rows, teacher_rows, prototypes, crop_image, crop_global):
    sizes = (*student_rows.shape, teacher_rows.shape[0], prototypes.shape[1])
    if fits(lax.axis_size("dp"), lax.axis_size("proto"), *sizes):
        return fused(student_rows, teacher_rows, prototypes, crop_image, crop_global)
    total_protos = lax.axis_size("proto") * prototypes.shape[1]
    img_local = teacher_rows.shape[0] // GLOBALS
    teach_total = lax.axis_size("dp") * teacher_rows.shape[0]
    weights = prototypes.astype(jnp.float32)
    col_scale = lax.rsqrt(jnp.sum(weights * weights, axis=0, keepdims=True) + 1e-06)
    w_norm = weights * col_scale
    w_bf = w_norm.astype(jnp.bfloat16)
    t_norm, t_scale = unit_rows(teacher_rows.astype(jnp.float32))
    t_bf = t_norm.astype(jnp.bfloat16)
    q_mat = jnp.exp(jnp.dot(t_bf, w_bf, preferred_element_type=jnp.float32) / 0.07)
    for step in range(ITERS):
        q_mat = q_mat / lax.psum(jnp.sum(q_mat, axis=0), "dp")[None, :] / total_protos
        row_tot = lax.psum(jnp.sum(q_mat, axis=1), "proto")
        q_mat = q_mat / row_tot[:, None] / teach_total
    targets = q_mat * teach_total
    x_norm, x_scale = unit_rows(student_rows.astype(jnp.float32))
    x_bf = x_norm.astype(jnp.bfloat16)
    logits = jnp.dot(x_bf, w_bf, preferred_element_type=jnp.float32) / 0.1
    expo = jnp.exp(logits)
    total = lax.psum(jnp.sum(expo, axis=1), "proto")
    probs = expo / total[:, None]
    image_here = crop_image - lax.axis_index("dp") * img_local
    first = jnp.take(targets, GLOBALS * image_here, axis=0)
    second = jnp.take(targets, GLOBALS * image_here + 1, axis=0)
    keep_first = (crop_global != 0).astype(jnp.float32)[:, None]
    keep_second = (crop_global != 1).astype(jnp.float32)[:, None]
    target_rows = first * keep_first + second * keep_second
    count = keep_first + keep_second
    scale_out = total_protos / 64.0
    grad_bf = (scale_out * (count * probs - target_rows) / 0.1).astype(jnp.bfloat16)
    crops_here = grad_bf.shape[0]
    groups = lax.axis_size("proto")
    share = -(-crops_here // groups)
    dxn_share = lax.psum_scatter(
        lax.dot_general(
            grad_bf, w_bf, (((1,), (1,)), ((), ())), preferred_element_type=jnp.float32
        ),
        "proto",
        scatter_dimension=0,
        tiled=True,
    )
    begin = lax.axis_index("proto") * share
    xn_share = lax.dynamic_slice_in_dim(x_norm, begin, share, 0)
    xr_share = lax.dynamic_slice_in_dim(x_scale, begin, share, 0)
    dx_share = xr_share * (
        dxn_share - xn_share * jnp.sum(xn_share * dxn_share, axis=1, keepdims=True)
    )
    student_grad = lax.all_gather(dx_share, "proto", axis=0, tiled=True)
    dwn_local = lax.dot_general(
        x_bf, grad_bf, (((0,), (0,)), ((), ())), preferred_element_type=jnp.float32
    )
    dwn_total = lax.psum(dwn_local, "dp")
    proto_grad = col_scale * (
        dwn_total - w_norm * jnp.sum(w_norm * dwn_total, axis=0, keepdims=True)
    )
    return (student_grad, proto_grad)


def solution(mesh):
    placed = (P("dp", None), P("dp", None), P(None, "proto"), P("dp"), P("dp"))
    return jax.shard_map(
        on_device,
        mesh=mesh,
        in_specs=placed,
        out_specs=(P("dp", None), P(None, "proto")),
        check_vma=False,
    )
```
